1024 devices in a mesh: row: 32 (over y_lo, x), col: 32 (over y_hi, z, core).
Axes of the slice: x: 8, y: 8 (y_hi: 2, y_lo: 4; y = y_hi * 4 + y_lo), z: 8, core: 2. Of those that a mesh axis runs over, the one named last changes fastest.
Arguments:
- amplitudes: bfloat16 [12288, 32768], P(('row', 'col')), may hold values from -12 to 12
- integrals: bfloat16 [32768, 2048], P(('row', 'col')), may hold values from -0.03125 to 0.03125
- pair_list: int32 [12288, 2], P(('row', 'col')), may hold values from 0 to 199
- block_sizes: int32 [8], replicated, may hold values from 104 to 128, as said below
- occ_energy: float32 [200], replicated, may hold values from -2 to -0.4
- virt_energy: float32 [128], replicated, may hold values from 0.3 to 2
Outputs:
- update: float32 [12288, 2048], P(('row', 'col'))
The draws below stay inside these ranges and needn't reach their ends.
Inputs may be any that keep to these rules, and one draw needn't show every extreme that they name: `block_sizes`: the entries sum to 1000; entries 0, 1 and 7 are below 128, and at least one other entry equals 128.
All inputs are finite; a program needn't handle non-finite values.
Results may differ from the reference program's by a relative error of at most 0.0003.
Values may be sent and summed in bfloat16 or wider, within the bound.
No kernel may reach another device: no remote copies, remote signals or barrier semaphores. Data moves between devices by JAX's collectives and lax.ppermute only.
A program may use at most 32 MiB of HBM per device.

```python
import jax
import jax.numpy as jnp

NIRREP = 8
NV = 128
VIRT = 1000
NOCC = 200
CD = 32768
AB = 2048
PAIRS = 12288


def draw_block_sizes(key, part):
    key = jax.random.fold_in(key, 11)
    spare = NIRREP * NV - VIRT
    key_full, key_units = jax.random.split(key)
    full_block = jax.random.randint(key_full, (), 2, NIRREP - 1)
    units = jax.random.randint(key_units, (spare - 3,), 0, NIRREP - 1)
    targets = units + (units >= full_block).astype(jnp.int32)
    labels = jnp.arange(NIRREP, dtype=jnp.int32)
    counts = jnp.sum((targets[:, None] == labels[None, :]).astype(jnp.int32), axis=0)
    base = ((labels == 0) | (labels == 1) | (labels == NIRREP - 1)).astype(jnp.int32)
    return (NV - counts - base).astype(jnp.int32)


def plant(values, stream_key, smallest, top_value):
    place = [jax.random.randint(jax.random.fold_in(stream_key, axis), (), 0, length) for axis, length in enumerate(values.shape)]
    main_axis = values.shape.index(max(values.shape))
    next_to = place[:main_axis] + [(place[main_axis] + 1) % values.shape[main_axis]] + place[main_axis + 1:]
    return values.at[tuple(place)].set(smallest).at[tuple(next_to)].set(top_value)


def block_scale(rng, shape, pieces, least, high):
    factor_of = 1.0
    for dim, shards_of in pieces:
        heights = jax.random.uniform(jax.random.fold_in(jax.random.fold_in(rng, 6), dim), (shards_of,), jnp.float32, least / len(pieces), high / len(pieces))
        factor_of = factor_of * jnp.repeat(jnp.exp(heights), shape[dim] // shards_of).reshape((-1,) + (1,) * (len(shape) - 1 - dim))
    return factor_of


def bell_draw(own_key, extent, deviation, limit, pieces=(), kind=jnp.bfloat16):
    drawn = jax.random.normal(own_key, extent, jnp.float32) * deviation
    if len(pieces) > 0:
        drawn = block_scale(own_key, extent, pieces, -0.22, 0.18) * drawn
    return jnp.clip(drawn, min=-limit, max=limit).astype(kind)


def setup_inputs(seed: int = 0) -> dict:
    seeds = jax.random.split(jax.random.key(seed), 7)
    return {
        "amplitudes": bell_draw(seeds[0], (PAIRS, CD), 2.0, 12.0, ((0, 1024),)),
        "integrals": bell_draw(seeds[1], (CD, AB), CD ** -0.5, 0.03125, ((0, 1024),)),
        "pair_list": plant(jax.random.randint(seeds[2], (PAIRS, 2), 0, NOCC), jax.random.fold_in(seeds[2], 1), 0, NOCC - 1).astype(jnp.int32),
        "block_sizes": draw_block_sizes(jax.random.fold_in(seeds[6], 71), 0),
        "occ_energy": jnp.clip(jax.random.uniform(seeds[4], (NOCC,), jnp.float32, -2.0, -0.4), -2.0, -0.4),
        "virt_energy": jnp.clip(jax.random.uniform(seeds[5], (NV,), jnp.float32, 0.3, 2.0), 0.3, 2.0),
    }


def reference(amplitudes, integrals, pair_list, block_sizes, occ_energy, virt_energy):
    pair_index = jnp.arange(CD, dtype=jnp.int32)
    irrep_index = pair_index // (NV * NV)
    first_virt = (pair_index // NV) % NV
    second_virt = pair_index % NV
    size_here = block_sizes[irrep_index]
    live_rows = (first_virt < size_here) & (second_virt < size_here)
    masked_integrals = jnp.where(live_rows[:, None], integrals, jnp.zeros((), jnp.bfloat16))
    ladder = jnp.dot(amplitudes, masked_integrals, preferred_element_type=jnp.float32)
    pair_energy = occ_energy[pair_list[:, 0]] + occ_energy[pair_list[:, 1]]
    out_index = jnp.arange(AB, dtype=jnp.int32)
    outer_virt = out_index // NV
    inner_virt = out_index % NV
    denominator = pair_energy[:, None] - virt_energy[outer_virt][None, :] - virt_energy[inner_virt][None, :]
    live_column = inner_virt < block_sizes[NIRREP - 1]
    return jnp.where(live_column[None, :], ladder / denominator, jnp.float32(0.0))
```

```python
import jax
import jax.numpy as jnp
from jax import lax
from jax.sharding import Mesh, PartitionSpec as P

NIRREP = 8
NV = 128
AXES = ("ylo", "x", "yhi", "z", "core")
PLANE = ("yhi", "ylo", "x")


def table_lookup(indices, table, table_length):
    matches = indices[..., None] == jnp.arange(table_length, dtype=jnp.int32)
    return jnp.sum(jnp.where(matches, table, jnp.zeros((), table.dtype)), axis=-1)


def local(amplitudes, integrals, pair_list, block_sizes, occ_energy, virt_energy):
    size = {axis: lax.axis_size(axis) for axis in AXES}
    pairs_local, summed = amplitudes.shape
    slab_rows, out_width = integrals.shape
    half = out_width // size["core"]

    halves = integrals.reshape(slab_rows, size["core"], half).transpose(1, 0, 2)
    swapped = lax.all_to_all(halves, "core", split_axis=0, concat_axis=0, tiled=True)
    panel = lax.all_gather(
        swapped.reshape(size["core"] * slab_rows, half), PLANE, axis=0, tiled=True
    )

    pair_index = jnp.arange(summed, dtype=jnp.int32)
    size_here = jnp.where(pair_index < NV * NV, block_sizes[0], block_sizes[1])
    live = (pair_index // NV % NV < size_here) & (pair_index % NV < size_here)
    masked = jnp.where(live[None, :], amplitudes, jnp.zeros((), jnp.bfloat16))
    blocked = masked.reshape(
        pairs_local, size["ylo"], size["x"], size["yhi"], size["z"], size["core"] * slab_rows
    ).transpose(4, 0, 3, 1, 2, 5)
    blocked = blocked.reshape(size["z"], pairs_local, summed // size["z"])
    columns = lax.all_to_all(blocked, "z", split_axis=0, concat_axis=0, tiled=True)
    both = lax.all_gather(columns, "core", axis=1, tiled=True)
    lhs = both.reshape(size["z"] * size["core"] * pairs_local, summed // size["z"])

    partial_value = jnp.dot(lhs, panel, preferred_element_type=jnp.float32)
    partial_value = partial_value.reshape(size["z"], size["core"] * pairs_local, half)
    reduced = lax.psum_scatter(partial_value, "z", scatter_dimension=0, tiled=False)
    reduced = reduced.reshape(size["core"], pairs_local, half)
    joined = lax.all_to_all(reduced, "core", split_axis=0, concat_axis=0, tiled=True)
    ladder = joined.transpose(1, 0, 2).reshape(pairs_local, out_width)

    pair_energy = jnp.sum(table_lookup(pair_list, occ_energy, occ_energy.shape[0]), axis=1)
    out_index = jnp.arange(out_width, dtype=jnp.int32)
    outer_virt = out_index // NV
    inner_virt = out_index % NV
    outer_energy = table_lookup(outer_virt, virt_energy, NV)
    inner_energy = table_lookup(inner_virt, virt_energy, NV)
    denominator = pair_energy[:, None] - outer_energy[None, :] - inner_energy[None, :]
    live_column = inner_virt < block_sizes[NIRREP - 1]
    return jnp.where(live_column[None, :], ladder / denominator, jnp.float32(0.0))


def solution(mesh):
    fine = Mesh(mesh.devices.reshape(4, 8, 2, 8, 2), AXES)
    split = P(AXES, None)
    return jax.shard_map(
        local,
        mesh=fine,
        in_specs=(split, split, split, P(), P(), P()),
        out_specs=split,
        check_vma=False,
    )
```

```python
import jax
import jax.numpy as jnp
from jax import lax
from jax.sharding import Mesh, PartitionSpec as P

NIRREP = 8
NV = 128
AXES = ("ylo", "x", "yhi", "zhi", "zlo", "core")
RING = ("yhi", "ylo")
SWAP = [(0, 1), (1, 0)]


def table_lookup(indices, table, table_length):
    matches = indices[..., None] == jnp.arange(table_length, dtype=jnp.int32)
    return jnp.sum(jnp.where(matches, table, jnp.zeros((), table.dtype)), axis=-1)


def local(amplitudes, integrals, pair_list, block_sizes, occ_energy, virt_energy):
    size = {axis: lax.axis_size(axis) for axis in AXES}
    pairs_local, summed = amplitudes.shape
    slab_rows, out_width = integrals.shape
    parts = size["zlo"] * size["core"]
    quarter = out_width // parts
    stripe = size["zhi"] * size["zlo"] * size["core"] * slab_rows

    quarters = integrals.reshape(slab_rows, parts, quarter).transpose(1, 0, 2)
    quarters = jnp.tile(quarters, (size["zhi"], 1, 1))
    rows = lax.all_to_all(quarters, ("zhi", "zlo", "core"), split_axis=0, concat_axis=0, tiled=True)
    panel = lax.all_gather(rows.reshape(stripe, quarter), RING, axis=0, tiled=True)

    pair_index = jnp.arange(summed, dtype=jnp.int32)
    size_here = jnp.where(pair_index < NV * NV, block_sizes[0], block_sizes[1])
    live = (pair_index // NV % NV < size_here) & (pair_index % NV < size_here)
    masked = jnp.where(live[None, :], amplitudes, jnp.zeros((), jnp.bfloat16))
    blocked = masked.reshape(pairs_local, size["ylo"], size["x"], size["yhi"], stripe)
    blocked = blocked.transpose(2, 3, 0, 1, 4)
    blocked = blocked.reshape(size["x"], 1, size["yhi"] * pairs_local, size["ylo"] * stripe)
    blocked = jnp.tile(blocked, (1, size["zlo"], 1, 1))
    groups = size["x"] * size["zlo"]
    blocked = blocked.reshape(groups, size["yhi"] * pairs_local, size["ylo"] * stripe)
    own = lax.all_to_all(blocked, ("x", "zlo"), split_axis=0, concat_axis=0, tiled=True)
    other = lax.ppermute(own, "core", SWAP)
    lhs = jnp.stack([own, other], axis=1)
    lhs = lhs.reshape(groups, size["core"], size["yhi"], pairs_local, size["ylo"] * stripe)
    lhs = lhs.transpose(0, 1, 3, 2, 4).reshape(groups * size["core"] * pairs_local, -1)

    partial_value = jnp.dot(lhs, panel, preferred_element_type=jnp.float32)
    partial_value = partial_value.reshape(groups, size["core"] * pairs_local, quarter)
    pieces = lax.all_to_all(partial_value, ("x", "zlo"), split_axis=0, concat_axis=0, tiled=True)
    pieces = pieces.reshape(size["x"], size["zlo"], size["core"], pairs_local, quarter)
    reduced = jnp.sum(pieces, axis=0)
    mine, theirs = reduced[:, 0], reduced[:, 1]
    arrived = lax.ppermute(theirs, "core", SWAP)
    first = lax.axis_index("core") == 0
    low = jnp.where(first, mine, arrived)
    high = jnp.where(first, arrived, mine)
    ladder = jnp.stack([low, high], axis=1).reshape(parts, pairs_local, quarter)
    ladder = ladder.transpose(1, 0, 2).reshape(pairs_local, out_width)

    pair_energy = jnp.sum(table_lookup(pair_list, occ_energy, occ_energy.shape[0]), axis=1)
    out_index = jnp.arange(out_width, dtype=jnp.int32)
    outer_virt = out_index // NV
    inner_virt = out_index % NV
    outer_energy = table_lookup(outer_virt, virt_energy, NV)
    inner_energy = table_lookup(inner_virt, virt_energy, NV)
    denominator = pair_energy[:, None] - outer_energy[None, :] - inner_energy[None, :]
    live_column = inner_virt < block_sizes[NIRREP - 1]
    return jnp.where(live_column[None, :], ladder / denominator, jnp.float32(0.0))


def solution(mesh):
    fine = Mesh(mesh.devices.reshape(4, 8, 2, 4, 2, 2), AXES)
    split = P(AXES, None)
    return jax.shard_map(
        local,
        mesh=fine,
        in_specs=(split, split, split, P(), P(), P()),
        out_specs=split,
        check_vma=False,
    )
```

```python
import functools

import jax
import jax.numpy as jnp
from jax import lax
from jax.experimental import pallas as pl
from jax.experimental.pallas import tpu as pltpu
from jax.sharding import Mesh, PartitionSpec as P

NIRREP = 8
NV = 128
AXES = ("ylo", "x", "yhi", "zhi", "zlo", "core")
RING = ("yhi", "ylo")
SWAP = [(0, 1), (1, 0)]
RING_COLUMNS = 128


def table_lookup(indices, table, table_length):
    matches = indices[..., None] == jnp.arange(table_length, dtype=jnp.int32)
    return jnp.sum(jnp.where(matches, table, jnp.zeros((), table.dtype)), axis=-1)


def ring_blocks(block, yhi, ylo):
    length = yhi * ylo

    def flat(place):
        return place % length % ylo * yhi + place % length // ylo

    def move(value, shift):
        pairs = [(flat(place), flat(place + shift)) for place in range(length)]
        return lax.ppermute(value, ("ylo", "yhi"), pairs)

    up = [block]
    down = [block]
    for step in range(length // 2):
        up.append(move(up[-1], 1))
        if step < length // 2 - 1:
            down.append(move(down[-1], -1))
    return jnp.stack(up + down[:0:-1])


def multiply_kernel(pairs, place_ref, own_ref, other_ref, panel_ref, ring_ref, out_ref, sums):
    half = pl.program_id(0)
    length, stripe, _ = ring_ref.shape
    wide = panel_ref.shape[1]
    width = out_ref.shape[1]
    blocks = own_ref.shape[1] // stripe
    for side, lhs_ref in enumerate((own_ref, other_ref)):
        sums[2 * side + half, :, :wide] = jnp.dot(
            lhs_ref[...], panel_ref[...], preferred_element_type=jnp.float32
        )
        total = jnp.zeros((lhs_ref.shape[0], width - wide), jnp.float32)
        for block in range(blocks):
            entry = lax.rem(place_ref[0] - (half * blocks + block) + length, length)
            total += jnp.dot(
                lhs_ref[:, block * stripe : (block + 1) * stripe],
                ring_ref[entry],
                preferred_element_type=jnp.float32,
            )
        sums[2 * side + half, :, wide:] = total

    @pl.when(half == 1)
    def _():
        for start in range(0, out_ref.shape[0], 2 * pairs):
            first = slice(start, start + pairs)
            second = slice(start + pairs, start + 2 * pairs)
            out_ref[first, :] = sums[0, first, :] + sums[1, second, :]
            out_ref[second, :] = sums[2, first, :] + sums[3, second, :]


def multiply(own, other, panel, ring, place, pairs):
    rows, half_depth = own.shape
    depth, wide = panel.shape
    width = wide + ring.shape[2]
    return pl.pallas_call(
        functools.partial(multiply_kernel, pairs),
        grid=(depth // half_depth,),
        out_shape=jax.ShapeDtypeStruct((rows, width), jnp.float32),
        in_specs=[
            pl.BlockSpec(memory_space=pltpu.SMEM),
            pl.BlockSpec((rows, half_depth), lambda k: (0, 0)),
            pl.BlockSpec((rows, half_depth), lambda k: (0, 0)),
            pl.BlockSpec((half_depth, wide), lambda k: (k, 0)),
            pl.BlockSpec(ring.shape, lambda k: (0, 0, 0)),
        ],
        out_specs=pl.BlockSpec((rows, width), lambda k: (0, 0)),
        scratch_shapes=[pltpu.VMEM((4, rows, width), jnp.float32)],
        compiler_params=pltpu.CompilerParams(
            dimension_semantics=("arbitrary",), vmem_limit_bytes=56 * 1024 * 1024
        ),
        cost_estimate=pl.CostEstimate(
            flops=4 * rows * depth * width,
            bytes_accessed=2 * (rows + width) * depth + 4 * rows * width,
            transcendentals=0,
        ),
        name="multiply",
    )(place.reshape(1), own, other, panel, ring)


def local(amplitudes, integrals, pair_list, block_sizes, occ_energy, virt_energy):
    size = {axis: lax.axis_size(axis) for axis in AXES}
    pairs_local, summed = amplitudes.shape
    slab_rows, out_width = integrals.shape
    parts = size["zlo"] * size["core"]
    quarter = out_width // parts
    stripe = size["zhi"] * size["zlo"] * size["core"] * slab_rows

    quarters = integrals.reshape(slab_rows, parts, quarter).transpose(1, 0, 2)
    quarters = jnp.tile(quarters, (size["zhi"], 1, 1))
    rows = lax.all_to_all(quarters, ("zhi", "zlo", "core"), split_axis=0, concat_axis=0, tiled=True)

    pair_index = jnp.arange(summed, dtype=jnp.int32)
    size_here = jnp.where(pair_index < NV * NV, block_sizes[0], block_sizes[1])
    live = (pair_index // NV % NV < size_here) & (pair_index % NV < size_here)
    masked = jnp.where(live[None, :], amplitudes, jnp.zeros((), jnp.bfloat16))
    blocked = masked.reshape(pairs_local, size["ylo"], size["x"], size["yhi"], stripe)
    blocked = blocked.transpose(2, 3, 0, 1, 4)
    blocked = blocked.reshape(size["x"], 1, size["yhi"] * pairs_local, size["ylo"] * stripe)
    blocked = jnp.tile(blocked, (1, size["zlo"], 1, 1))
    groups = size["x"] * size["zlo"]
    blocked = blocked.reshape(groups, size["yhi"] * pairs_local, size["ylo"] * stripe)
    rows, blocked = lax.optimization_barrier((rows, blocked))
    rows = rows.reshape(stripe, quarter)
    wide = quarter - RING_COLUMNS
    panel = lax.all_gather(rows[:, :wide], RING, axis=0, tiled=True)
    own = lax.all_to_all(blocked, ("x", "zlo"), split_axis=0, concat_axis=0, tiled=True)
    ring = ring_blocks(rows[:, wide:], size["yhi"], size["ylo"])
    own, ring = lax.optimization_barrier((own, ring))
    own = own.reshape(groups * size["yhi"] * pairs_local, size["ylo"] * stripe)
    other = lax.ppermute(own, "core", SWAP)
    place = lax.axis_index("yhi") * size["ylo"] + lax.axis_index("ylo")
    partial_value = multiply(own, other, panel, ring, place, pairs_local)
    partial_value = partial_value.reshape(groups, size["core"] * pairs_local, quarter)
    pieces = lax.all_to_all(partial_value, ("x", "zlo"), split_axis=0, concat_axis=0, tiled=True)
    pieces = pieces.reshape(size["x"], size["zlo"], size["core"], pairs_local, quarter)
    reduced = jnp.sum(pieces, axis=0)
    mine, theirs = reduced[:, 0], reduced[:, 1]
    arrived = lax.ppermute(theirs, "core", SWAP)
    first = lax.axis_index("core") == 0
    low = jnp.where(first, mine, arrived)
    high = jnp.where(first, arrived, mine)
    ladder = jnp.stack([low, high], axis=1).reshape(parts, pairs_local, quarter)
    ladder = ladder.transpose(1, 0, 2).reshape(pairs_local, out_width)

    pair_energy = jnp.sum(table_lookup(pair_list, occ_energy, occ_energy.shape[0]), axis=1)
    out_index = jnp.arange(out_width, dtype=jnp.int32)
    outer_virt = out_index // NV
    inner_virt = out_index % NV
    outer_energy = table_lookup(outer_virt, virt_energy, NV)
    inner_energy = table_lookup(inner_virt, virt_energy, NV)
    denominator = pair_energy[:, None] - outer_energy[None, :] - inner_energy[None, :]
    live_column = inner_virt < block_sizes[NIRREP - 1]
    return jnp.where(live_column[None, :], ladder / denominator, jnp.float32(0.0))


def solution(mesh):
    fine = Mesh(mesh.devices.reshape(4, 8, 2, 4, 2, 2), AXES)
    split = P(AXES, None)
    return jax.shard_map(
        local,
        mesh=fine,
        in_specs=(split, split, split, P(), P(), P()),
        out_specs=split,
        check_vma=False,
    )
```

```python
import functools

import jax
import jax.numpy as jnp
from jax import lax
from jax.experimental import pallas as pl
from jax.experimental.pallas import tpu as pltpu
from jax.sharding import Mesh, PartitionSpec as P

NIRREP = 8
NV = 128
AXES = ("ylo", "x", "yhi", "zhi", "zlo", "core")
RING = ("yhi", "ylo")
SWAP = [(0, 1), (1, 0)]


def table_lookup(indices, table, table_length):
    matches = indices[..., None] == jnp.arange(table_length, dtype=jnp.int32)
    return jnp.sum(jnp.where(matches, table, jnp.zeros((), table.dtype)), axis=-1)


def spread_kernel(parts, copies, x_ref, out_ref):
    width = out_ref.shape[2]
    for part in range(parts):
        value = x_ref[:, part * width : (part + 1) * width]
        for copy in range(copies):
            out_ref[copy * parts + part] = value


def spread_quarters(integrals, parts, copies):
    rows, width = integrals.shape
    return pl.pallas_call(
        functools.partial(spread_kernel, parts, copies),
        out_shape=jax.ShapeDtypeStruct((parts * copies, rows, width // parts), integrals.dtype),
        in_specs=[pl.BlockSpec(memory_space=pltpu.VMEM)],
        out_specs=pl.BlockSpec(memory_space=pltpu.VMEM),
        cost_estimate=pl.CostEstimate(
            flops=0, bytes_accessed=2 * rows * width * (1 + copies), transcendentals=0
        ),
        name="spread_quarters",
    )(integrals)


def assemble_kernel(pairs, own_ref, other_ref, out_ref):
    depth = own_ref.shape[2]
    halves = own_ref.shape[1] // pairs
    for group in range(own_ref.shape[0]):
        for half in range(halves):
            rows = slice(half * pairs, (half + 1) * pairs)
            both = jnp.concatenate(
                [ref[group].astype(jnp.float32)[rows] for ref in (own_ref, other_ref)], axis=0
            )
            out_ref[group, :, half * depth : (half + 1) * depth] = both.astype(out_ref.dtype)


def assemble(own, other, pairs):
    groups, rows, depth = own.shape
    halves = rows // pairs
    block = pl.BlockSpec((4, rows, depth), lambda g: (g, 0, 0))
    return pl.pallas_call(
        functools.partial(assemble_kernel, pairs),
        grid=(groups // 4,),
        out_shape=jax.ShapeDtypeStruct((groups, 2 * pairs, halves * depth), own.dtype),
        in_specs=[block, block],
        out_specs=pl.BlockSpec((4, 2 * pairs, halves * depth), lambda g: (g, 0, 0)),
        compiler_params=pltpu.CompilerParams(vmem_limit_bytes=16 * 1024 * 1024),
        cost_estimate=pl.CostEstimate(
            flops=2 * own.size, bytes_accessed=8 * own.size, transcendentals=0
        ),
        name="assemble",
    )(own, other)


def multiply_kernel(lhs_ref, panel_ref, out_ref):
    product = jnp.dot(lhs_ref[...], panel_ref[...], preferred_element_type=jnp.float32)

    @pl.when(pl.program_id(0) == 0)
    def _():
        out_ref[...] = product

    @pl.when(pl.program_id(0) > 0)
    def _():
        out_ref[...] += product


def multiply(lhs, panel):
    rows, depth = lhs.shape
    width = panel.shape[1]
    block = 1024
    return pl.pallas_call(
        multiply_kernel,
        grid=(depth // block,),
        out_shape=jax.ShapeDtypeStruct((rows, width), jnp.float32),
        in_specs=[
            pl.BlockSpec((rows, block), lambda k: (0, k)),
            pl.BlockSpec((block, width), lambda k: (k, 0)),
        ],
        out_specs=pl.BlockSpec((rows, width), lambda k: (0, 0)),
        compiler_params=pltpu.CompilerParams(
            dimension_semantics=("arbitrary",), vmem_limit_bytes=56 * 1024 * 1024
        ),
        cost_estimate=pl.CostEstimate(
            flops=2 * rows * depth * width,
            bytes_accessed=2 * (rows + width) * depth + 4 * rows * width,
            transcendentals=0,
        ),
        name="multiply",
    )(lhs, panel)


def local(amplitudes, integrals, pair_list, block_sizes, occ_energy, virt_energy):
    size = {axis: lax.axis_size(axis) for axis in AXES}
    pairs_local, summed = amplitudes.shape
    slab_rows, out_width = integrals.shape
    parts = size["zlo"] * size["core"]
    quarter = out_width // parts
    stripe = size["zhi"] * size["zlo"] * size["core"] * slab_rows

    quarters = spread_quarters(integrals, parts, size["zhi"])
    rows = lax.all_to_all(quarters, ("zhi", "zlo", "core"), split_axis=0, concat_axis=0, tiled=True)

    pair_index = jnp.arange(summed, dtype=jnp.int32)
    size_here = jnp.where(pair_index < NV * NV, block_sizes[0], block_sizes[1])
    live = (pair_index // NV % NV < size_here) & (pair_index % NV < size_here)
    masked = jnp.where(live[None, :], amplitudes, jnp.zeros((), jnp.bfloat16))
    blocked = masked.reshape(pairs_local, size["ylo"], size["x"], size["yhi"], stripe)
    blocked = blocked.transpose(2, 3, 0, 1, 4)
    blocked = blocked.reshape(size["x"], size["yhi"] * pairs_local, size["ylo"] * stripe)
    rows, blocked = lax.optimization_barrier((rows, blocked))
    panel = lax.all_gather(rows.reshape(stripe, quarter), RING, axis=0, tiled=True)
    groups = size["x"] * size["zlo"]
    blocked = jnp.broadcast_to(blocked[:, None], (size["x"], size["zlo"]) + blocked.shape[1:])
    blocked = blocked.reshape((groups,) + blocked.shape[2:])
    own = lax.all_to_all(blocked, ("x", "zlo"), split_axis=0, concat_axis=0, tiled=True)
    other = lax.ppermute(own, "core", SWAP)
    lhs = assemble(own, other, pairs_local)
    partial_value = multiply(lhs.reshape(groups * size["core"] * pairs_local, -1), panel)
    partial_value = partial_value.reshape(groups, size["core"] * pairs_local, quarter)
    pieces = lax.all_to_all(partial_value, ("x", "zlo"), split_axis=0, concat_axis=0, tiled=True)
    pieces = pieces.reshape(size["x"], size["zlo"], size["core"], pairs_local, quarter)
    reduced = jnp.sum(pieces, axis=0)
    mine, theirs = reduced[:, 0], reduced[:, 1]
    arrived = lax.ppermute(theirs, "core", SWAP)
    first = lax.axis_index("core") == 0
    low = jnp.where(first, mine, arrived)
    high = jnp.where(first, arrived, mine)
    ladder = jnp.stack([low, high], axis=1).reshape(parts, pairs_local, quarter)
    ladder = ladder.transpose(1, 0, 2).reshape(pairs_local, out_width)

    pair_energy = jnp.sum(table_lookup(pair_list, occ_energy, occ_energy.shape[0]), axis=1)
    out_index = jnp.arange(out_width, dtype=jnp.int32)
    outer_virt = out_index // NV
    inner_virt = out_index % NV
    outer_energy = table_lookup(outer_virt, virt_energy, NV)
    inner_energy = table_lookup(inner_virt, virt_energy, NV)
    denominator = pair_energy[:, None] - outer_energy[None, :] - inner_energy[None, :]
    live_column = inner_virt < block_sizes[NIRREP - 1]
    return jnp.where(live_column[None, :], ladder / denominator, jnp.float32(0.0))


def solution(mesh):
    fine = Mesh(mesh.devices.reshape(4, 8, 2, 4, 2, 2), AXES)
    split = P(AXES, None)
    return jax.shard_map(
        local,
        mesh=fine,
        in_specs=(split, split, split, P(), P(), P()),
        out_specs=split,
        check_vma=False,
    )
```

```python
import functools

import jax
import jax.numpy as jnp
from jax import lax
from jax.experimental import pallas as pl
from jax.experimental.pallas import tpu as pltpu
from jax.sharding import Mesh, PartitionSpec as P

NIRREP = 8
NV = 128
AXES = ("ylo", "x", "yhi", "zhi", "zlo", "core")
RING = ("yhi", "ylo")
SWAP = [(0, 1), (1, 0)]


def table_lookup(indices, table, table_length):
    matches = indices[..., None] == jnp.arange(table_length, dtype=jnp.int32)
    return jnp.sum(jnp.where(matches, table, jnp.zeros((), table.dtype)), axis=-1)


def spread_kernel(parts, copies, x_ref, out_ref):
    width = out_ref.shape[2]
    for part in range(parts):
        value = x_ref[:, part * width : (part + 1) * width]
        for copy in range(copies):
            out_ref[copy * parts + part] = value


def spread_quarters(integrals, parts, copies):
    rows, width = integrals.shape
    return pl.pallas_call(
        functools.partial(spread_kernel, parts, copies),
        out_shape=jax.ShapeDtypeStruct((parts * copies, rows, width // parts), integrals.dtype),
        in_specs=[pl.BlockSpec(memory_space=pltpu.VMEM)],
        out_specs=pl.BlockSpec(memory_space=pltpu.VMEM),
        cost_estimate=pl.CostEstimate(
            flops=0, bytes_accessed=2 * rows * width * (1 + copies), transcendentals=0
        ),
        name="spread_quarters",
    )(integrals)


def assemble_kernel(pairs, own_ref, other_ref, out_ref):
    depth = own_ref.shape[2]
    halves = own_ref.shape[1] // pairs
    for group in range(own_ref.shape[0]):
        for half in range(halves):
            rows = slice(half * pairs, (half + 1) * pairs)
            both = jnp.concatenate(
                [ref[group].astype(jnp.float32)[rows] for ref in (own_ref, other_ref)], axis=0
            )
            out_ref[group, :, half * depth : (half + 1) * depth] = both.astype(out_ref.dtype)


def assemble(own, other, pairs):
    groups, rows, depth = own.shape
    halves = rows // pairs
    block = pl.BlockSpec((4, rows, depth), lambda g: (g, 0, 0))
    return pl.pallas_call(
        functools.partial(assemble_kernel, pairs),
        grid=(groups // 4,),
        out_shape=jax.ShapeDtypeStruct((groups, 2 * pairs, halves * depth), own.dtype),
        in_specs=[block, block],
        out_specs=pl.BlockSpec((4, 2 * pairs, halves * depth), lambda g: (g, 0, 0)),
        compiler_params=pltpu.CompilerParams(vmem_limit_bytes=16 * 1024 * 1024),
        cost_estimate=pl.CostEstimate(
            flops=2 * own.size, bytes_accessed=8 * own.size, transcendentals=0
        ),
        name="assemble",
    )(own, other)


def multiply_kernel(block, lhs_ref, panel_ref, out_ref, left, right, arrived):
    copies = []
    for index, start in enumerate(range(0, panel_ref.shape[0], block)):
        span = pl.ds(start, block)
        pair = (
            pltpu.make_async_copy(lhs_ref.at[:, span], left.at[:, span], arrived.at[index, 0]),
            pltpu.make_async_copy(panel_ref.at[span], right.at[span], arrived.at[index, 1]),
        )
        for copy in pair:
            copy.start()
        copies.append(pair)
    for index, pair in enumerate(copies):
        for copy in pair:
            copy.wait()
        span = slice(index * block, (index + 1) * block)
        product = jnp.dot(left[:, span], right[span, :], preferred_element_type=jnp.float32)
        if index == 0:
            out_ref[...] = product
        else:
            out_ref[...] += product


def multiply(lhs, panel):
    rows, depth = lhs.shape
    width = panel.shape[1]
    block = 512
    return pl.pallas_call(
        functools.partial(multiply_kernel, block),
        out_shape=jax.ShapeDtypeStruct((rows, width), jnp.float32),
        in_specs=[pl.BlockSpec(memory_space=pl.ANY)] * 2,
        out_specs=pl.BlockSpec(memory_space=pltpu.VMEM),
        scratch_shapes=[
            pltpu.VMEM((rows, depth), lhs.dtype),
            pltpu.VMEM((depth, width), panel.dtype),
            pltpu.SemaphoreType.DMA((depth // block, 2)),
        ],
        compiler_params=pltpu.CompilerParams(vmem_limit_bytes=56 * 1024 * 1024),
        cost_estimate=pl.CostEstimate(
            flops=2 * rows * depth * width,
            bytes_accessed=2 * (rows + width) * depth + 4 * rows * width,
            transcendentals=0,
        ),
        name="multiply",
    )(lhs, panel)


def local(amplitudes, integrals, pair_list, block_sizes, occ_energy, virt_energy):
    size = {axis: lax.axis_size(axis) for axis in AXES}
    pairs_local, summed = amplitudes.shape
    slab_rows, out_width = integrals.shape
    parts = size["zlo"] * size["core"]
    quarter = out_width // parts
    stripe = size["zhi"] * size["zlo"] * size["core"] * slab_rows

    quarters = spread_quarters(integrals, parts, size["zhi"])
    rows = lax.all_to_all(quarters, ("zhi", "zlo", "core"), split_axis=0, concat_axis=0, tiled=True)

    pair_index = jnp.arange(summed, dtype=jnp.int32)
    size_here = jnp.where(pair_index < NV * NV, block_sizes[0], block_sizes[1])
    live = (pair_index // NV % NV < size_here) & (pair_index % NV < size_here)
    masked = jnp.where(live[None, :], amplitudes, jnp.zeros((), jnp.bfloat16))
    blocked = masked.reshape(pairs_local, size["ylo"], size["x"], size["yhi"], stripe)
    blocked = blocked.transpose(2, 3, 0, 1, 4)
    blocked = blocked.reshape(size["x"], size["yhi"] * pairs_local, size["ylo"] * stripe)
    rows, blocked = lax.optimization_barrier((rows, blocked))
    panel = lax.all_gather(rows.reshape(stripe, quarter), RING, axis=0, tiled=True)
    groups = size["x"] * size["zlo"]
    blocked = jnp.broadcast_to(blocked[:, None], (size["x"], size["zlo"]) + blocked.shape[1:])
    blocked = blocked.reshape((groups,) + blocked.shape[2:])
    own = lax.all_to_all(blocked, ("x", "zlo"), split_axis=0, concat_axis=0, tiled=True)
    other = lax.ppermute(own, "core", SWAP)
    lhs = assemble(own, other, pairs_local)
    partial_value = multiply(lhs.reshape(groups * size["core"] * pairs_local, -1), panel)
    partial_value = partial_value.reshape(groups, size["core"] * pairs_local, quarter)
    pieces = lax.all_to_all(partial_value, ("x", "zlo"), split_axis=0, concat_axis=0, tiled=True)
    pieces = pieces.reshape(size["x"], size["zlo"], size["core"], pairs_local, quarter)
    reduced = jnp.sum(pieces, axis=0)
    mine, theirs = reduced[:, 0], reduced[:, 1]
    arrived = lax.ppermute(theirs, "core", SWAP)
    first = lax.axis_index("core") == 0
    low = jnp.where(first, mine, arrived)
    high = jnp.where(first, arrived, mine)
    ladder = jnp.stack([low, high], axis=1).reshape(parts, pairs_local, quarter)
    ladder = ladder.transpose(1, 0, 2).reshape(pairs_local, out_width)

    pair_energy = jnp.sum(table_lookup(pair_list, occ_energy, occ_energy.shape[0]), axis=1)
    out_index = jnp.arange(out_width, dtype=jnp.int32)
    outer_virt = out_index // NV
    inner_virt = out_index % NV
    outer_energy = table_lookup(outer_virt, virt_energy, NV)
    inner_energy = table_lookup(inner_virt, virt_energy, NV)
    denominator = pair_energy[:, None] - outer_energy[None, :] - inner_energy[None, :]
    live_column = inner_virt < block_sizes[NIRREP - 1]
    return jnp.where(live_column[None, :], ladder / denominator, jnp.float32(0.0))


def solution(mesh):
    fine = Mesh(mesh.devices.reshape(4, 8, 2, 4, 2, 2), AXES)
    split = P(AXES, None)
    return jax.shard_map(
        local,
        mesh=fine,
        in_specs=(split, split, split, P(), P(), P()),
        out_specs=split,
        check_vma=False,
    )
```

```python
import functools

import jax
import jax.numpy as jnp
from jax import lax
from jax.experimental import pallas as pl
from jax.experimental.pallas import tpu as pltpu
from jax.sharding import Mesh, PartitionSpec as P

NIRREP = 8
NV = 128
AXES = ("ylo", "x", "yhi", "zhi", "zlo", "core")
RING = ("yhi", "ylo")
SWAP = [(0, 1), (1, 0)]


def table_lookup(indices, table, table_length):
    matches = indices[..., None] == jnp.arange(table_length, dtype=jnp.int32)
    return jnp.sum(jnp.where(matches, table, jnp.zeros((), table.dtype)), axis=-1)


def spread_kernel(parts, x_ref, out_ref, done):
    width = out_ref.shape[2]
    copies = []
    for index in range(out_ref.shape[0]):
        start = index % parts * width
        copies.append(
            pltpu.make_async_copy(
                x_ref.at[:, pl.ds(start, width)], out_ref.at[index], done.at[index]
            )
        )
        copies[-1].start()
    for copy in copies:
        copy.wait()


def spread_quarters(integrals, parts, copies):
    rows, width = integrals.shape
    return pl.pallas_call(
        functools.partial(spread_kernel, parts),
        out_shape=jax.ShapeDtypeStruct((parts * copies, rows, width // parts), integrals.dtype),
        in_specs=[pl.BlockSpec(memory_space=pl.ANY)],
        out_specs=pl.BlockSpec(memory_space=pl.ANY),
        scratch_shapes=[pltpu.SemaphoreType.DMA((parts * copies,))],
        cost_estimate=pl.CostEstimate(
            flops=0, bytes_accessed=2 * rows * width * (1 + copies), transcendentals=0
        ),
        name="spread_quarters",
    )(integrals)


def assemble_kernel(pairs, own_ref, other_ref, out_ref):
    depth = own_ref.shape[2]
    halves = own_ref.shape[1] // pairs
    for group in range(own_ref.shape[0]):
        for half in range(halves):
            rows = slice(half * pairs, (half + 1) * pairs)
            both = jnp.concatenate(
                [ref[group].astype(jnp.float32)[rows] for ref in (own_ref, other_ref)], axis=0
            )
            out_ref[group, :, half * depth : (half + 1) * depth] = both.astype(out_ref.dtype)


def assemble(own, other, pairs):
    groups, rows, depth = own.shape
    halves = rows // pairs
    block = pl.BlockSpec((4, rows, depth), lambda g: (g, 0, 0))
    return pl.pallas_call(
        functools.partial(assemble_kernel, pairs),
        grid=(groups // 4,),
        out_shape=jax.ShapeDtypeStruct((groups, 2 * pairs, halves * depth), own.dtype),
        in_specs=[block, block],
        out_specs=pl.BlockSpec((4, 2 * pairs, halves * depth), lambda g: (g, 0, 0)),
        compiler_params=pltpu.CompilerParams(vmem_limit_bytes=16 * 1024 * 1024),
        cost_estimate=pl.CostEstimate(
            flops=2 * own.size, bytes_accessed=8 * own.size, transcendentals=0
        ),
        name="assemble",
    )(own, other)


def multiply_kernel(
    block, pairs, core_ref, lhs_ref, panel_ref, out_ref, left, right, total, arrived
):
    copies = []
    for index, start in enumerate(range(0, panel_ref.shape[0], block)):
        span = pl.ds(start, block)
        pair = (
            pltpu.make_async_copy(lhs_ref.at[:, span], left.at[:, span], arrived.at[index, 0]),
            pltpu.make_async_copy(panel_ref.at[span], right.at[span], arrived.at[index, 1]),
        )
        for copy in pair:
            copy.start()
        copies.append(pair)
    for index, pair in enumerate(copies):
        for copy in pair:
            copy.wait()
        span = slice(index * block, (index + 1) * block)
        product = jnp.dot(left[:, span], right[span, :], preferred_element_type=jnp.float32)
        if index == 0:
            total[...] = product
        else:
            total[...] += product

    width = out_ref.shape[2]
    for group in range(out_ref.shape[0] // 2):
        for side in range(2):
            device = 2 * group + (core_ref[0] if side == 0 else 1 - core_ref[0])
            start = (2 * group + side) * pairs
            for part in range(total.shape[1] // width):
                out_ref[device, part * pairs : (part + 1) * pairs, :] = total[
                    start : start + pairs, part * width : (part + 1) * width
                ]


def multiply(lhs, panel, core, pairs):
    rows, depth = lhs.shape
    width = panel.shape[1]
    block = 512
    return pl.pallas_call(
        functools.partial(multiply_kernel, block, pairs),
        out_shape=jax.ShapeDtypeStruct((rows // pairs, 2 * pairs, width // 2), jnp.float32),
        in_specs=[pl.BlockSpec(memory_space=pltpu.SMEM)]
        + [pl.BlockSpec(memory_space=pl.ANY)] * 2,
        out_specs=pl.BlockSpec(memory_space=pltpu.VMEM),
        scratch_shapes=[
            pltpu.VMEM((rows, depth), lhs.dtype),
            pltpu.VMEM((depth, width), panel.dtype),
            pltpu.VMEM((rows, width), jnp.float32),
            pltpu.SemaphoreType.DMA((depth // block, 2)),
        ],
        compiler_params=pltpu.CompilerParams(vmem_limit_bytes=56 * 1024 * 1024),
        cost_estimate=pl.CostEstimate(
            flops=2 * rows * depth * width,
            bytes_accessed=2 * (rows + width) * depth + 4 * rows * width,
            transcendentals=0,
        ),
        name="multiply",
    )(core.reshape(1), lhs, panel)


def local(amplitudes, integrals, pair_list, block_sizes, occ_energy, virt_energy):
    size = {axis: lax.axis_size(axis) for axis in AXES}
    pairs_local, summed = amplitudes.shape
    slab_rows, out_width = integrals.shape
    parts = size["zlo"] * size["core"]
    quarter = out_width // parts
    stripe = size["zhi"] * size["zlo"] * size["core"] * slab_rows

    quarters = spread_quarters(integrals, parts, size["zhi"])
    rows = lax.all_to_all(quarters, ("zhi", "zlo", "core"), split_axis=0, concat_axis=0, tiled=True)

    pair_index = jnp.arange(summed, dtype=jnp.int32)
    size_here = jnp.where(pair_index < NV * NV, block_sizes[0], block_sizes[1])
    live = (pair_index // NV % NV < size_here) & (pair_index % NV < size_here)
    masked = jnp.where(live[None, :], amplitudes, jnp.zeros((), jnp.bfloat16))
    blocked = masked.reshape(pairs_local, size["ylo"], size["x"], size["yhi"], stripe)
    blocked = blocked.transpose(2, 3, 0, 1, 4)
    blocked = blocked.reshape(size["x"], size["yhi"] * pairs_local, size["ylo"] * stripe)
    rows, blocked = lax.optimization_barrier((rows, blocked))
    panel = lax.all_gather(rows.reshape(stripe, quarter), RING, axis=0, tiled=True)
    groups = size["x"] * size["zlo"]
    blocked = jnp.broadcast_to(blocked[:, None], (size["x"], size["zlo"]) + blocked.shape[1:])
    blocked = blocked.reshape((groups,) + blocked.shape[2:])
    own = lax.all_to_all(blocked, ("x", "zlo"), split_axis=0, concat_axis=0, tiled=True)
    other = lax.ppermute(own, "core", SWAP)
    lhs = assemble(own, other, pairs_local)
    lhs = lhs.reshape(groups * size["core"] * pairs_local, -1)
    partial_value = multiply(lhs, panel, lax.axis_index("core"), pairs_local)
    pieces = lax.all_to_all(
        partial_value, ("x", "zlo", "core"), split_axis=0, concat_axis=0, tiled=True
    )
    ladder = jnp.sum(pieces.reshape((size["x"], parts) + pieces.shape[1:]), axis=0)
    ladder = ladder.reshape(parts, 2, pairs_local, quarter // 2)
    ladder = ladder.transpose(2, 0, 1, 3).reshape(pairs_local, out_width)

    pair_energy = jnp.sum(table_lookup(pair_list, occ_energy, occ_energy.shape[0]), axis=1)
    out_index = jnp.arange(out_width, dtype=jnp.int32)
    outer_virt = out_index // NV
    inner_virt = out_index % NV
    outer_energy = table_lookup(outer_virt, virt_energy, NV)
    inner_energy = table_lookup(inner_virt, virt_energy, NV)
    denominator = pair_energy[:, None] - outer_energy[None, :] - inner_energy[None, :]
    live_column = inner_virt < block_sizes[NIRREP - 1]
    return jnp.where(live_column[None, :], ladder / denominator, jnp.float32(0.0))


def solution(mesh):
    fine = Mesh(mesh.devices.reshape(4, 8, 2, 4, 2, 2), AXES)
    split = P(AXES, None)
    return jax.shard_map(
        local,
        mesh=fine,
        in_specs=(split, split, split, P(), P(), P()),
        out_specs=split,
        check_vma=False,
    )
```

```python
import functools

import jax
import jax.numpy as jnp
from jax import lax
from jax.experimental import pallas as pl
from jax.experimental.pallas import tpu as pltpu
from jax.sharding import Mesh, PartitionSpec as P

NIRREP = 8
NV = 128
AXES = ("ylo", "x", "yhi", "zhi", "zlo", "core")
RING = ("yhi", "ylo")
SWAP = [(0, 1), (1, 0)]


def table_lookup(indices, table, table_length):
    matches = indices[..., None] == jnp.arange(table_length, dtype=jnp.int32)
    return jnp.sum(jnp.where(matches, table, jnp.zeros((), table.dtype)), axis=-1)


def spread_kernel(parts, copies, x_ref, out_ref):
    width = out_ref.shape[2]
    for part in range(parts):
        value = x_ref[:, part * width : (part + 1) * width]
        for copy in range(copies):
            out_ref[copy * parts + part] = value


def spread_quarters(integrals, parts, copies):
    rows, width = integrals.shape
    return pl.pallas_call(
        functools.partial(spread_kernel, parts, copies),
        out_shape=jax.ShapeDtypeStruct((parts * copies, rows, width // parts), integrals.dtype),
        in_specs=[pl.BlockSpec(memory_space=pltpu.VMEM)],
        out_specs=pl.BlockSpec(memory_space=pltpu.VMEM),
        cost_estimate=pl.CostEstimate(
            flops=0, bytes_accessed=2 * rows * width * (1 + copies), transcendentals=0
        ),
        name="spread_quarters",
    )(integrals)


def assemble_kernel(pairs, own_ref, other_ref, out_ref):
    depth = own_ref.shape[2]
    halves = own_ref.shape[1] // pairs
    for group in range(own_ref.shape[0]):
        for half in range(halves):
            rows = slice(half * pairs, (half + 1) * pairs)
            both = jnp.concatenate(
                [ref[group].astype(jnp.float32)[rows] for ref in (own_ref, other_ref)], axis=0
            )
            out_ref[group, :, half * depth : (half + 1) * depth] = both.astype(out_ref.dtype)


def assemble(own, other, pairs):
    groups, rows, depth = own.shape
    halves = rows // pairs
    block = pl.BlockSpec((4, rows, depth), lambda g: (g, 0, 0))
    return pl.pallas_call(
        functools.partial(assemble_kernel, pairs),
        grid=(groups // 4,),
        out_shape=jax.ShapeDtypeStruct((groups, 2 * pairs, halves * depth), own.dtype),
        in_specs=[block, block],
        out_specs=pl.BlockSpec((4, 2 * pairs, halves * depth), lambda g: (g, 0, 0)),
        compiler_params=pltpu.CompilerParams(vmem_limit_bytes=16 * 1024 * 1024),
        cost_estimate=pl.CostEstimate(
            flops=2 * own.size, bytes_accessed=8 * own.size, transcendentals=0
        ),
        name="assemble",
    )(own, other)


def multiply_kernel(
    block, pairs, core_ref, lhs_ref, panel_ref, out_ref, left, right, total, arrived
):
    copies = []
    for index, start in enumerate(range(0, panel_ref.shape[0], block)):
        span = pl.ds(start, block)
        pair = (
            pltpu.make_async_copy(lhs_ref.at[:, span], left.at[:, span], arrived.at[index, 0]),
            pltpu.make_async_copy(panel_ref.at[span], right.at[span], arrived.at[index, 1]),
        )
        for copy in pair:
            copy.start()
        copies.append(pair)
    for index, pair in enumerate(copies):
        for copy in pair:
            copy.wait()
        span = slice(index * block, (index + 1) * block)
        product = jnp.dot(left[:, span], right[span, :], preferred_element_type=jnp.float32)
        if index == 0:
            total[...] = product
        else:
            total[...] += product

    width = out_ref.shape[2]
    for group in range(out_ref.shape[0] // 2):
        for side in range(2):
            device = 2 * group + (core_ref[0] if side == 0 else 1 - core_ref[0])
            start = (2 * group + side) * pairs
            for part in range(total.shape[1] // width):
                out_ref[device, part * pairs : (part + 1) * pairs, :] = total[
                    start : start + pairs, part * width : (part + 1) * width
                ]


def multiply(lhs, panel, core, pairs):
    rows, depth = lhs.shape
    width = panel.shape[1]
    block = 512
    return pl.pallas_call(
        functools.partial(multiply_kernel, block, pairs),
        out_shape=jax.ShapeDtypeStruct((rows // pairs, 2 * pairs, width // 2), jnp.float32),
        in_specs=[pl.BlockSpec(memory_space=pltpu.SMEM)]
        + [pl.BlockSpec(memory_space=pl.ANY)] * 2,
        out_specs=pl.BlockSpec(memory_space=pltpu.VMEM),
        scratch_shapes=[
            pltpu.VMEM((rows, depth), lhs.dtype),
            pltpu.VMEM((depth, width), panel.dtype),
            pltpu.VMEM((rows, width), jnp.float32),
            pltpu.SemaphoreType.DMA((depth // block, 2)),
        ],
        compiler_params=pltpu.CompilerParams(vmem_limit_bytes=48 * 1024 * 1024),
        cost_estimate=pl.CostEstimate(
            flops=2 * rows * depth * width,
            bytes_accessed=2 * (rows + width) * depth + 4 * rows * width,
            transcendentals=0,
        ),
        name="multiply",
    )(core.reshape(1), lhs, panel)


def local(amplitudes, integrals, pair_list, block_sizes, occ_energy, virt_energy):
    size = {axis: lax.axis_size(axis) for axis in AXES}
    pairs_local, summed = amplitudes.shape
    slab_rows, out_width = integrals.shape
    parts = size["zlo"] * size["core"]
    quarter = out_width // parts
    stripe = size["zhi"] * size["zlo"] * size["core"] * slab_rows

    quarters = spread_quarters(integrals, parts, size["zhi"])
    rows = lax.all_to_all(quarters, ("zhi", "zlo", "core"), split_axis=0, concat_axis=0, tiled=True)

    pair_index = jnp.arange(summed, dtype=jnp.int32)
    size_here = jnp.where(pair_index < NV * NV, block_sizes[0], block_sizes[1])
    live = (pair_index // NV % NV < size_here) & (pair_index % NV < size_here)
    masked = jnp.where(live[None, :], amplitudes, jnp.zeros((), jnp.bfloat16))
    blocked = masked.reshape(pairs_local, size["ylo"], size["x"], size["yhi"], stripe)
    blocked = blocked.transpose(2, 3, 0, 1, 4)
    blocked = blocked.reshape(size["x"], size["yhi"] * pairs_local, size["ylo"] * stripe)
    rows, blocked = lax.optimization_barrier((rows, blocked))
    panel = lax.all_gather(rows.reshape(stripe, quarter), RING, axis=0, tiled=True)
    groups = size["x"] * size["zlo"]
    blocked = jnp.broadcast_to(blocked[:, None], (size["x"], size["zlo"]) + blocked.shape[1:])
    blocked = blocked.reshape((groups,) + blocked.shape[2:])
    own = lax.all_to_all(blocked, ("x", "zlo"), split_axis=0, concat_axis=0, tiled=True)
    other = lax.ppermute(own, "core", SWAP)
    lhs = assemble(own, other, pairs_local)
    lhs = lhs.reshape(groups * size["core"] * pairs_local, -1)
    partial_value = multiply(lhs, panel, lax.axis_index("core"), pairs_local)
    pieces = lax.all_to_all(
        partial_value, ("x", "zlo", "core"), split_axis=0, concat_axis=0, tiled=True
    )
    ladder = jnp.sum(pieces.reshape((size["x"], parts) + pieces.shape[1:]), axis=0)
    ladder = ladder.reshape(parts, 2, pairs_local, quarter // 2)
    ladder = ladder.transpose(2, 0, 1, 3).reshape(pairs_local, out_width)

    pair_energy = jnp.sum(table_lookup(pair_list, occ_energy, occ_energy.shape[0]), axis=1)
    out_index = jnp.arange(out_width, dtype=jnp.int32)
    outer_virt = out_index // NV
    inner_virt = out_index % NV
    outer_energy = table_lookup(outer_virt, virt_energy, NV)
    inner_energy = table_lookup(inner_virt, virt_energy, NV)
    denominator = pair_energy[:, None] - outer_energy[None, :] - inner_energy[None, :]
    live_column = inner_virt < block_sizes[NIRREP - 1]
    return jnp.where(live_column[None, :], ladder / denominator, jnp.float32(0.0))


def solution(mesh):
    fine = Mesh(mesh.devices.reshape(4, 8, 2, 4, 2, 2), AXES)
    split = P(AXES, None)
    return jax.shard_map(
        local,
        mesh=fine,
        in_specs=(split, split, split, P(), P(), P()),
        out_specs=split,
        check_vma=False,
    )
```

```python
import functools

import jax
import jax.numpy as jnp
from jax import lax
from jax.experimental import pallas as pl
from jax.experimental.pallas import tpu as pltpu
from jax.sharding import Mesh, PartitionSpec as P

NIRREP = 8
NV = 128
AXES = ("ylo", "x", "yhi", "zhi", "zlo", "core")
SWAP = [(0, 1), (1, 0)]


def table_lookup(indices, table, table_length):
    matches = indices[..., None] == jnp.arange(table_length, dtype=jnp.int32)
    return jnp.sum(jnp.where(matches, table, jnp.zeros((), table.dtype)), axis=-1)


def spread_kernel(parts, copies, x_ref, out_ref):
    width = out_ref.shape[2]
    for part in range(parts):
        value = x_ref[:, part * width : (part + 1) * width]
        for copy in range(copies):
            out_ref[copy * parts + part] = value


def spread_quarters(integrals, parts, copies):
    rows, width = integrals.shape
    return pl.pallas_call(
        functools.partial(spread_kernel, parts, copies),
        out_shape=jax.ShapeDtypeStruct((parts * copies, rows, width // parts), integrals.dtype),
        in_specs=[pl.BlockSpec(memory_space=pltpu.VMEM)],
        out_specs=pl.BlockSpec(memory_space=pltpu.VMEM),
        cost_estimate=pl.CostEstimate(
            flops=0, bytes_accessed=2 * rows * width * (1 + copies), transcendentals=0
        ),
        name="spread_quarters",
    )(integrals)


def assemble_kernel(pairs, own_ref, other_ref, out_ref):
    depth = own_ref.shape[2]
    halves = own_ref.shape[1] // pairs
    for group in range(own_ref.shape[0]):
        for half in range(halves):
            rows = slice(half * pairs, (half + 1) * pairs)
            both = jnp.concatenate(
                [ref[group].astype(jnp.float32)[rows] for ref in (own_ref, other_ref)], axis=0
            )
            out_ref[group, :, half * depth : (half + 1) * depth] = both.astype(out_ref.dtype)


def assemble(own, other, pairs):
    groups, rows, depth = own.shape
    halves = rows // pairs
    block = pl.BlockSpec((4, rows, depth), lambda g: (g, 0, 0))
    return pl.pallas_call(
        functools.partial(assemble_kernel, pairs),
        grid=(groups // 4,),
        out_shape=jax.ShapeDtypeStruct((groups, 2 * pairs, halves * depth), own.dtype),
        in_specs=[block, block],
        out_specs=pl.BlockSpec((4, 2 * pairs, halves * depth), lambda g: (g, 0, 0)),
        compiler_params=pltpu.CompilerParams(vmem_limit_bytes=8 * 1024 * 1024),
        cost_estimate=pl.CostEstimate(
            flops=2 * own.size, bytes_accessed=8 * own.size, transcendentals=0
        ),
        name="assemble",
    )(own, other)


def ring_move(yhi, ylo, value, shift):
    length = yhi * ylo

    def flat(place):
        return place % length % ylo * yhi + place % length // ylo

    pairs = [(flat(place), flat(place + shift)) for place in range(length)]
    return lax.ppermute(value, ("ylo", "yhi"), pairs)


def multiply_kernel(
    order, length, pairs, place_ref, core_ref, lhs_ref, *refs
):
    near_refs, far_refs, (out_ref, total) = refs[: len(order)], refs[len(order) : -2], refs[-2:]
    stripe = near_refs[0].shape[0]
    entries = [(0, shift, ref) for shift, ref in zip(order, near_refs)]
    entries += [
        (index * ref.shape[1], length // 2, ref) for index, ref in enumerate(far_refs)
    ]
    for column, shift, block_ref in entries:
        source = lax.rem(place_ref[0] - shift + length, length)
        lanes = pl.ds(pl.multiple_of(source * stripe, stripe), stripe)
        product = jnp.dot(lhs_ref[:, lanes], block_ref[...], preferred_element_type=jnp.float32)
        columns = slice(column, column + block_ref.shape[1])
        if shift == 0:
            total[:, columns] = product
        else:
            total[:, columns] += product

    width = out_ref.shape[2]
    for group in range(out_ref.shape[0] // 2):
        for side in range(2):
            device = 2 * group + (core_ref[0] if side == 0 else 1 - core_ref[0])
            start = (2 * group + side) * pairs
            for part in range(total.shape[1] // width):
                out_ref[device, part * pairs : (part + 1) * pairs, :] = total[
                    start : start + pairs, part * width : (part + 1) * width
                ]


def multiply(lhs, near, far, order, length, place, core, pairs):
    rows, depth = lhs.shape
    width = near[0].shape[1]
    return pl.pallas_call(
        functools.partial(multiply_kernel, order, length, pairs),
        out_shape=jax.ShapeDtypeStruct((rows // pairs, 2 * pairs, width // 2), jnp.float32),
        in_specs=[pl.BlockSpec(memory_space=pltpu.SMEM)] * 2
        + [pl.BlockSpec(memory_space=pltpu.VMEM)] * (1 + len(near) + len(far)),
        out_specs=pl.BlockSpec(memory_space=pltpu.VMEM),
        scratch_shapes=[pltpu.VMEM((rows, width), jnp.float32)],
        compiler_params=pltpu.CompilerParams(vmem_limit_bytes=12 * 1024 * 1024),
        cost_estimate=pl.CostEstimate(
            flops=2 * rows * depth * width,
            bytes_accessed=2 * (rows + width) * depth + 4 * rows * width,
            transcendentals=0,
        ),
        name="multiply",
    )(place.reshape(1), core.reshape(1), lhs, *near, *far)


def local(amplitudes, integrals, pair_list, block_sizes, occ_energy, virt_energy):
    size = {axis: lax.axis_size(axis) for axis in AXES}
    pairs_local, summed = amplitudes.shape
    slab_rows, out_width = integrals.shape
    parts = size["zlo"] * size["core"]
    quarter = out_width // parts
    stripe = size["zhi"] * size["zlo"] * size["core"] * slab_rows

    quarters = spread_quarters(integrals, parts, size["zhi"])
    rows = lax.all_to_all(quarters, ("zhi", "zlo", "core"), split_axis=0, concat_axis=0, tiled=True)

    pair_index = jnp.arange(summed, dtype=jnp.int32)
    size_here = jnp.where(pair_index < NV * NV, block_sizes[0], block_sizes[1])
    live = (pair_index // NV % NV < size_here) & (pair_index % NV < size_here)
    masked = jnp.where(live[None, :], amplitudes, jnp.zeros((), jnp.bfloat16))
    blocked = masked.reshape(pairs_local, size["ylo"], size["x"], size["yhi"], stripe)
    blocked = blocked.transpose(2, 3, 0, 1, 4)
    blocked = blocked.reshape(size["x"], size["yhi"] * pairs_local, size["ylo"] * stripe)
    rows, blocked = lax.optimization_barrier((rows, blocked))
    groups = size["x"] * size["zlo"]
    blocked = jnp.broadcast_to(blocked[:, None], (size["x"], size["zlo"]) + blocked.shape[1:])
    blocked = blocked.reshape((groups,) + blocked.shape[2:])
    own = lax.all_to_all(blocked, ("x", "zlo"), split_axis=0, concat_axis=0, tiled=True)
    length = size["yhi"] * size["ylo"]
    move = functools.partial(ring_move, size["yhi"], size["ylo"])
    ring = {0: rows.reshape(stripe, quarter)}
    for step in range(1, length // 2):
        for sign in (1, -1):
            ring[sign * step] = move(ring[sign * (step - 1)], sign)
    order = sorted(ring, key=abs)
    near = [ring[shift] for shift in order]
    ends = (ring[length // 2 - 1][:, : quarter // 2], ring[1 - length // 2][:, quarter // 2 :])
    own, ends = lax.optimization_barrier((own, ends))
    far = [move(end, sign) for end, sign in zip(ends, (1, -1))]
    other = lax.ppermute(own, "core", SWAP)
    lhs = assemble(own, other, pairs_local)
    lhs = lhs.reshape(groups * size["core"] * pairs_local, -1)
    place = lax.axis_index("yhi") * size["ylo"] + lax.axis_index("ylo")
    partial_value = multiply(lhs, near, far, order, length, place, lax.axis_index("core"), pairs_local)
    pieces = lax.all_to_all(
        partial_value, ("x", "zlo", "core"), split_axis=0, concat_axis=0, tiled=True
    )
    ladder = jnp.sum(pieces.reshape((size["x"], parts) + pieces.shape[1:]), axis=0)
    ladder = ladder.reshape(parts, 2, pairs_local, quarter // 2)
    ladder = ladder.transpose(2, 0, 1, 3).reshape(pairs_local, out_width)

    pair_energy = jnp.sum(table_lookup(pair_list, occ_energy, occ_energy.shape[0]), axis=1)
    out_index = jnp.arange(out_width, dtype=jnp.int32)
    outer_virt = out_index // NV
    inner_virt = out_index % NV
    outer_energy = table_lookup(outer_virt, virt_energy, NV)
    inner_energy = table_lookup(inner_virt, virt_energy, NV)
    denominator = pair_energy[:, None] - outer_energy[None, :] - inner_energy[None, :]
    live_column = inner_virt < block_sizes[NIRREP - 1]
    return jnp.where(live_column[None, :], ladder / denominator, jnp.float32(0.0))


def solution(mesh):
    fine = Mesh(mesh.devices.reshape(4, 8, 2, 4, 2, 2), AXES)
    split = P(AXES, None)
    return jax.shard_map(
        local,
        mesh=fine,
        in_specs=(split, split, split, P(), P(), P()),
        out_specs=split,
        check_vma=False,
    )
```

```python
import functools

import jax
import jax.numpy as jnp
from jax import lax
from jax.experimental import pallas as pl
from jax.experimental.pallas import tpu as pltpu
from jax.sharding import Mesh, PartitionSpec as P

NIRREP = 8
NV = 128
AXES = ("ylo", "x", "yhi", "za", "zb", "zc", "core")
SWAP = [(0, 1), (1, 0)]


def table_lookup(indices, table, table_length):
    matches = indices[..., None] == jnp.arange(table_length, dtype=jnp.int32)
    return jnp.sum(jnp.where(matches, table, jnp.zeros((), table.dtype)), axis=-1)


def spread_kernel(parts, copies, x_ref, out_ref):
    width = out_ref.shape[2]
    for part in range(parts):
        value = x_ref[:, part * width : (part + 1) * width]
        for copy in range(copies):
            out_ref[copy * parts + part] = value


def spread_quarters(integrals, parts, copies):
    rows, width = integrals.shape
    return pl.pallas_call(
        functools.partial(spread_kernel, parts, copies),
        out_shape=jax.ShapeDtypeStruct((parts * copies, rows, width // parts), integrals.dtype),
        in_specs=[pl.BlockSpec(memory_space=pltpu.VMEM)],
        out_specs=pl.BlockSpec(memory_space=pltpu.VMEM),
        cost_estimate=pl.CostEstimate(
            flops=0, bytes_accessed=2 * rows * width * (1 + copies), transcendentals=0
        ),
        name="spread_quarters",
    )(integrals)


def assemble_kernel(pairs, own_ref, other_ref, out_ref):
    depth = own_ref.shape[2]
    halves = own_ref.shape[1] // pairs
    for group in range(own_ref.shape[0]):
        for half in range(halves):
            rows = slice(half * pairs, (half + 1) * pairs)
            both = jnp.concatenate(
                [ref[group].astype(jnp.float32)[rows] for ref in (own_ref, other_ref)], axis=0
            )
            out_ref[group, :, half * depth : (half + 1) * depth] = both.astype(out_ref.dtype)


def assemble(own, other, pairs):
    groups, rows, depth = own.shape
    halves = rows // pairs
    block = pl.BlockSpec((4, rows, depth), lambda g: (g, 0, 0))
    return pl.pallas_call(
        functools.partial(assemble_kernel, pairs),
        grid=(groups // 4,),
        out_shape=jax.ShapeDtypeStruct((groups, 2 * pairs, halves * depth), own.dtype),
        in_specs=[block, block],
        out_specs=pl.BlockSpec((4, 2 * pairs, halves * depth), lambda g: (g, 0, 0)),
        compiler_params=pltpu.CompilerParams(vmem_limit_bytes=8 * 1024 * 1024),
        cost_estimate=pl.CostEstimate(
            flops=2 * own.size, bytes_accessed=8 * own.size, transcendentals=0
        ),
        name="assemble",
    )(own, other)


def ring_move(yhi, ylo, value, shift):
    length = yhi * ylo

    def flat(place):
        return place % length % ylo * yhi + place % length // ylo

    pairs = [(flat(place), flat(place + shift)) for place in range(length)]
    return lax.ppermute(value, ("ylo", "yhi"), pairs)


def multiply_kernel(
    order, length, pairs, place_ref, core_ref, lhs_ref, *refs
):
    near_refs, far_refs, (out_ref, total) = refs[: len(order)], refs[len(order) : -2], refs[-2:]
    stripe = near_refs[0].shape[0]
    entries = [(0, shift, ref) for shift, ref in zip(order, near_refs)]
    entries += [
        (index * ref.shape[1], length // 2, ref) for index, ref in enumerate(far_refs)
    ]
    for column, shift, block_ref in entries:
        source = lax.rem(place_ref[0] - shift + length, length)
        lanes = pl.ds(pl.multiple_of(source * stripe, stripe), stripe)
        product = jnp.dot(lhs_ref[:, lanes], block_ref[...], preferred_element_type=jnp.float32)
        columns = slice(column, column + block_ref.shape[1])
        if shift == 0:
            total[:, columns] = product
        else:
            total[:, columns] += product

    width = out_ref.shape[2]
    for group in range(out_ref.shape[0] // 2):
        for side in range(2):
            device = 2 * group + (core_ref[0] if side == 0 else 1 - core_ref[0])
            start = (2 * group + side) * pairs
            for part in range(total.shape[1] // width):
                out_ref[device, part * pairs : (part + 1) * pairs, :] = total[
                    start : start + pairs, part * width : (part + 1) * width
                ]


def multiply(lhs, near, far, order, length, place, core, pairs):
    rows, depth = lhs.shape
    width = near[0].shape[1]
    return pl.pallas_call(
        functools.partial(multiply_kernel, order, length, pairs),
        out_shape=jax.ShapeDtypeStruct((rows // pairs, 2 * pairs, width // 2), jnp.float32),
        in_specs=[pl.BlockSpec(memory_space=pltpu.SMEM)] * 2
        + [pl.BlockSpec(memory_space=pltpu.VMEM)] * (1 + len(near) + len(far)),
        out_specs=pl.BlockSpec(memory_space=pltpu.VMEM),
        scratch_shapes=[pltpu.VMEM((rows, width), jnp.float32)],
        compiler_params=pltpu.CompilerParams(vmem_limit_bytes=12 * 1024 * 1024),
        cost_estimate=pl.CostEstimate(
            flops=2 * rows * depth * width,
            bytes_accessed=2 * (rows + width) * depth + 4 * rows * width,
            transcendentals=0,
        ),
        name="multiply",
    )(place.reshape(1), core.reshape(1), lhs, *near, *far)


def local(amplitudes, integrals, pair_list, block_sizes, occ_energy, virt_energy):
    size = {axis: lax.axis_size(axis) for axis in AXES}
    pairs_local, summed = amplitudes.shape
    slab_rows, out_width = integrals.shape
    parts = size["zc"] * size["core"]
    quarter = out_width // parts
    slab = parts * slab_rows
    stripe = size["za"] * slab

    quarters = spread_quarters(integrals, parts, size["za"])
    rows = lax.all_to_all(quarters, ("za", "zc", "core"), split_axis=0, concat_axis=0, tiled=True)

    pair_index = jnp.arange(summed, dtype=jnp.int32)
    size_here = jnp.where(pair_index < NV * NV, block_sizes[0], block_sizes[1])
    live = (pair_index // NV % NV < size_here) & (pair_index % NV < size_here)
    masked = jnp.where(live[None, :], amplitudes, jnp.zeros((), jnp.bfloat16))
    blocked = masked.reshape(
        pairs_local, size["ylo"], size["x"], size["yhi"], size["za"], size["zb"], slab
    ).transpose(2, 5, 3, 0, 1, 4, 6)
    owners = size["x"] * size["zb"]
    blocked = blocked.reshape(owners, size["yhi"] * pairs_local, size["ylo"] * stripe)
    rows, blocked = lax.optimization_barrier((rows, blocked))
    groups = owners * size["zc"]
    blocked = jnp.broadcast_to(blocked[:, None], (owners, size["zc"]) + blocked.shape[1:])
    blocked = blocked.reshape((groups,) + blocked.shape[2:])
    own = lax.all_to_all(blocked, ("x", "zb", "zc"), split_axis=0, concat_axis=0, tiled=True)
    length = size["yhi"] * size["ylo"]
    move = functools.partial(ring_move, size["yhi"], size["ylo"])
    ring = {0: rows.reshape(stripe, quarter)}
    for step in range(1, length // 2):
        for sign in (1, -1):
            ring[sign * step] = move(ring[sign * (step - 1)], sign)
    order = sorted(ring, key=abs)
    near = [ring[shift] for shift in order]
    ends = (ring[length // 2 - 1][:, : quarter // 2], ring[1 - length // 2][:, quarter // 2 :])
    own, ends = lax.optimization_barrier((own, ends))
    far = [move(end, sign) for end, sign in zip(ends, (1, -1))]
    other = lax.ppermute(own, "core", SWAP)
    lhs = assemble(own, other, pairs_local)
    lhs = lhs.reshape(groups * size["core"] * pairs_local, -1)
    place = lax.axis_index("yhi") * size["ylo"] + lax.axis_index("ylo")
    partial_value = multiply(lhs, near, far, order, length, place, lax.axis_index("core"), pairs_local)
    pieces = lax.all_to_all(
        partial_value, ("x", "zb", "zc", "core"), split_axis=0, concat_axis=0, tiled=True
    )
    ladder = jnp.sum(pieces.reshape((owners, parts) + pieces.shape[1:]), axis=0)
    ladder = ladder.reshape(parts, 2, pairs_local, quarter // 2)
    ladder = ladder.transpose(2, 0, 1, 3).reshape(pairs_local, out_width)

    pair_energy = jnp.sum(table_lookup(pair_list, occ_energy, occ_energy.shape[0]), axis=1)
    out_index = jnp.arange(out_width, dtype=jnp.int32)
    outer_virt = out_index // NV
    inner_virt = out_index % NV
    outer_energy = table_lookup(outer_virt, virt_energy, NV)
    inner_energy = table_lookup(inner_virt, virt_energy, NV)
    denominator = pair_energy[:, None] - outer_energy[None, :] - inner_energy[None, :]
    live_column = inner_virt < block_sizes[NIRREP - 1]
    return jnp.where(live_column[None, :], ladder / denominator, jnp.float32(0.0))


def solution(mesh):
    fine = Mesh(mesh.devices.reshape(4, 8, 2, 2, 2, 2, 2), AXES)
    split = P(AXES, None)
    return jax.shard_map(
        local,
        mesh=fine,
        in_specs=(split, split, split, P(), P(), P()),
        out_specs=split,
        check_vma=False,
    )
```
